32 devices in a mesh: rep: 2 (over y), serve: 4 (over x, core), tp: 4 (over z).
Axes of the slice: x: 2, y: 2, z: 4, core: 2. Of those that a mesh axis runs over, the one named last changes fastest.
Arguments:
- hidden: bfloat16 [3072, 8192], P(('rep', 'serve', 'tp')), parts along dimension 0, may hold values from -6 to 6
- kv_weight: bfloat16 [8192, 2048], P('tp'), may hold values from -0.0625 to 0.0625
- a_store: bfloat16 [128, 8192, 64], P('serve', 'tp'), may hold values from -0.0625 to 0.0625
- b_store: bfloat16 [128, 64, 2048], P('serve', None, 'tp'), may hold values from -0.75 to 0.75
- home: int32 [256], P('rep'), parts along dimension 0, may hold values from 0 to 127, as said below
- wanted: int32 [8, 16], P('rep'), parts along dimension 0, may hold values from 0 to 127, as said below
- tile_slot: int32 [192], P(('rep', 'serve')), parts along dimension 0, may hold values from 0 to 15, as said below
Outputs:
- kv_out: bfloat16 [3072, 2048], P(('rep', 'serve'), 'tp'), parts along dimension 0
The draws below stay inside these ranges and needn't reach their ends.
There are 2 independent parts, one for each index of `rep`. The reference program is written for one: setup_inputs(seed, part) draws one part's arguments, and reference() takes and returns one part's arrays. A program takes and returns all parts, laid end to end along the dimension named above; an argument that names none is the same for every part. Nothing has to cross between parts.
Inputs may be any that keep to these rules, and one draw needn't show every extreme that they name: home is a permutation: adapter a sits in store row home[a]; store rows s * 32 to (s + 1) * 32 - 1 lie on serve index s. `wanted`: each group's 16 entries are distinct adapters; at most 4 of one group's entries sit on one serve index, and in every group exactly 4 sit on some serve index. `tile_slot`: the tiles of group g are tiles g * 24 to (g + 1) * 24 - 1; their entries never fall along the group, and every entry of the group's list is used by one tile or more.
All inputs are finite; a program needn't handle non-finite values.
Results may differ from the reference program's by a relative error of at most 0.001.
Values may be sent and summed in bfloat16 or wider, within the bound.
A program may use at most 128 MiB of HBM per device.

```python
import jax
import jax.numpy as jnp
from jax import lax

D = 8192
KVDIM = 1024
RANK = 64
TILE = 16
NEED = 16
ADP_DEV = 32
CAP = 4
ADAPTERS = 128
TILES_GRP = 24
TILES = 96
ROWS = 1536
N_SERVE = 4


def store_holder(key):
    return jax.random.permutation(key, ADP_DEV * N_SERVE).astype(jnp.int32)


def slot_table(key):
    return jax.random.permutation(key, ADP_DEV).astype(jnp.int32)


def draw_home(key, part):
    holder = store_holder(key)
    return jnp.argsort(holder, stable=True).astype(jnp.int32)


def draw_wanted(key, part):
    holder = store_holder(key)
    key = jax.random.fold_in(key, 11)
    key_hot, key_rest, key_shuffle, key_slots = jax.random.split(key, 4)
    hot_pair = jax.random.randint(key_hot, (2,), 0, N_SERVE).astype(jnp.int32)
    groups = jnp.arange(N_SERVE, dtype=jnp.int32)
    hot_store = jnp.where(groups % 2 == 0, hot_pair[0], hot_pair[1])
    pool_size = (N_SERVE - 1) * CAP

    def take_rest(sub_key):
        return jax.random.permutation(sub_key, pool_size)[:NEED - CAP].astype(jnp.int32)
    picked = jax.vmap(take_rest)(jax.random.split(key_rest, N_SERVE))
    others = picked // CAP
    others = others + (others >= hot_store[:, None]).astype(jnp.int32)
    stores = jnp.concatenate([jnp.broadcast_to(hot_store[:, None], (N_SERVE, CAP)), others], axis=1)

    def shuffle_row(sub_key):
        return jax.random.permutation(sub_key, NEED).astype(jnp.int32)
    shuffle = jax.vmap(shuffle_row)(jax.random.split(key_shuffle, N_SERVE))
    stores = jnp.take_along_axis(stores, shuffle, axis=1)
    same_store = (stores[:, :, None] == groups[None, None, :]).astype(jnp.int32)
    slot_rank = jnp.sum((jnp.cumsum(same_store, axis=1) - same_store) * same_store, axis=2)
    tables = jax.vmap(slot_table)(jax.random.split(key_slots, N_SERVE * N_SERVE))
    tables = tables.reshape(N_SERVE, N_SERVE, ADP_DEV)
    slots = tables[groups[:, None], stores, slot_rank]
    store_rows = stores * ADP_DEV + slots
    return holder[store_rows].astype(jnp.int32)


def draw_tile_slot(key, part):
    key = jax.random.fold_in(key, 23)
    extra_tiles = jax.random.randint(key, (N_SERVE, TILES_GRP - NEED), 0, NEED).astype(jnp.int32)
    first_tiles = jnp.broadcast_to(jnp.arange(NEED, dtype=jnp.int32), (N_SERVE, NEED))
    joined = jnp.concatenate([first_tiles, extra_tiles], axis=1)
    return jnp.sort(joined, axis=1).reshape(-1).astype(jnp.int32)


def level_of(stream_key, extent, shards, low, top_value):
    level, own = 1.0, jax.random.fold_in(stream_key, 6)
    for axis_at, shards_of in shards:
        heights = jnp.exp(jax.random.uniform(jax.random.fold_in(own, axis_at), (shards_of,), jnp.float32, low / len(shards), top_value / len(shards)))
        level = level * jnp.repeat(heights, extent[axis_at] // shards_of).reshape([-1 if axis == axis_at else 1 for axis in range(len(extent))])
    return level


def noise(key, shape, scale, limit, pieces=(), kind=jnp.bfloat16):
    drawn = scale * jax.random.normal(key, shape, jnp.float32)
    if pieces:
        drawn = drawn * level_of(key, shape, pieces, -0.22, 0.18)
    return jnp.clip(drawn, -limit, limit).astype(kind)


def setup_inputs(seed: int = 0, part: int = 0) -> dict:
    key_list = jax.random.split(jax.random.key(seed), 8)
    part_splits = jax.random.split(jax.random.fold_in(key_list[7], part), 8)
    return {
        "hidden": noise(part_splits[0], (ROWS, D), 1.0, 6.0, ((0, 16),)),
        "kv_weight": noise(key_list[1], (D, 2 * KVDIM), D ** -0.5, 0.0625, ((0, 4),)),
        "a_store": noise(key_list[2], (ADAPTERS, D, RANK), D ** -0.5, 0.0625, ((0, 4), (1, 4))),
        "b_store": noise(key_list[3], (ADAPTERS, RANK, 2 * KVDIM), RANK ** -0.5, 0.75, ((0, 4), (2, 4))),
        "home": draw_home(jax.random.fold_in(jax.random.fold_in(key_list[7], part), 71), part),
        "wanted": draw_wanted(jax.random.fold_in(jax.random.fold_in(key_list[7], part), 71), part),
        "tile_slot": draw_tile_slot(jax.random.fold_in(jax.random.fold_in(key_list[7], part), 71), part),
    }


adapter_scale = 0.5


def reference(hidden, kv_weight, a_store, b_store, home, wanted, tile_slot):
    base_output = jnp.dot(hidden, kv_weight, preferred_element_type=jnp.float32)
    tile_ids = jnp.arange(TILES, dtype=jnp.int32)
    tile_group = tile_ids // TILES_GRP
    adapter = wanted[tile_group, tile_slot]
    store_rows = home[adapter].astype(jnp.int32)
    tiled_rows = hidden.reshape(TILES, TILE, D)

    def one_tile(inputs):
        row_tile, store_row = inputs
        shrink_panel = lax.dynamic_index_in_dim(a_store, store_row, 0, keepdims=False)
        expand_panel = lax.dynamic_index_in_dim(b_store, store_row, 0, keepdims=False)
        reduced_rank_rows = jnp.dot(row_tile, shrink_panel, preferred_element_type=jnp.float32)
        return jnp.dot(reduced_rank_rows, expand_panel.astype(jnp.float32), precision=lax.Precision.HIGHEST)

    adapter_update = lax.map(one_tile, (tiled_rows, store_rows)).reshape(ROWS, 2 * KVDIM)
    return (base_output + adapter_scale * adapter_update).astype(jnp.bfloat16)
```

```python
import functools

import jax
import jax.numpy as jnp
from jax import lax
from jax.experimental import pallas as pl
from jax.experimental.pallas import tpu as pltpu
from jax.sharding import PartitionSpec as P

adapter_scale = 0.5
LEVELS = 32767.0


def flip(index, step, count):
    result, bit = 0, 1
    while bit < count:
        on = lax.rem(lax.div(index, jnp.int32(bit)), jnp.int32(2))
        if isinstance(step, int):
            turned = 1 - on if step & bit else on
        else:
            turned = lax.rem(on + lax.rem(lax.div(step, jnp.int32(bit)), jnp.int32(2)), jnp.int32(2))
        result = result + bit * turned
        bit *= 2
    return result


def quantize(values):
    top = jnp.maximum(jnp.max(jnp.abs(values)), 1e-30)
    coded = jnp.round(values * (LEVELS / top)).astype(jnp.int32).astype(jnp.int16)
    return coded, jnp.full((8, 128), top * (1.0 / LEVELS), jnp.float32)


def restore(coded, scale):
    return coded.astype(jnp.int32).astype(jnp.float32) * scale


def kernel(
    cfg,
    home, wanted, tile_slot, hidden, weight, a_store, b_store,
    out,
    xs, w_vm, a_vm, b_vm, send_a, send_b, got_a, got_b,
    p_send, p_scale_send, p_recv, p_scale_recv,
    l_send, l_scale_send, l_recv, l_scale_recv,
    own, row_slot, low_rows, picks, places,
    local_sem, x_send, x_recv, a_send, a_recv, bs_send, bs_recv,
    ps_send, ps_recv, psc_send, psc_recv,
    ls_send, ls_recv, lsc_send, lsc_recv,
):
    n_tp, n_serve, cap, held = cfg
    need = wanted.shape[1]
    tiles = tile_slot.shape[0]
    block, depth = xs.shape[1], xs.shape[2]
    rows = n_tp * block
    tile_rows = rows // tiles
    rank = a_vm.shape[1]
    feats = out.shape[1]
    half = rows // 2
    me = lax.axis_index("tp")
    group = lax.axis_index("serve")

    def x_copy(u):
        j = flip(me, u, n_tp)
        return pltpu.make_async_remote_copy(
            src_ref=hidden.at[:, pl.ds(pl.multiple_of(j * depth, depth), depth)],
            dst_ref=xs.at[u],
            send_sem=x_send.at[u], recv_sem=x_recv.at[u],
            device_id={"tp": j},
        )

    def panel_copy(src, dst, ssem, rsem, u, landing):
        d = flip(group, u, n_serve)
        return pltpu.make_async_remote_copy(
            src_ref=src.at[u], dst_ref=dst.at[landing],
            send_sem=ssem.at[u], recv_sem=rsem.at[u],
            device_id={"serve": d},
        )

    def part_copies(u, t):
        c = flip(me, u, n_tp)
        return (
            pltpu.make_async_remote_copy(
                src_ref=p_send.at[u, t], dst_ref=p_recv.at[u, t],
                send_sem=ps_send.at[u, t], recv_sem=ps_recv.at[u, t],
                device_id={"tp": c},
            ),
            pltpu.make_async_remote_copy(
                src_ref=p_scale_send.at[u, t], dst_ref=p_scale_recv.at[u, t],
                send_sem=psc_send.at[u, t], recv_sem=psc_recv.at[u, t],
                device_id={"tp": c},
            ),
        )

    def low_copies(u):
        c = flip(me, u, n_tp)
        return (
            pltpu.make_async_remote_copy(
                src_ref=l_send, dst_ref=l_recv.at[u],
                send_sem=ls_send.at[u], recv_sem=ls_recv.at[u],
                device_id={"tp": c},
            ),
            pltpu.make_async_remote_copy(
                src_ref=l_scale_send, dst_ref=l_scale_recv.at[u],
                send_sem=lsc_send.at[u], recv_sem=lsc_recv.at[u],
                device_id={"tp": c},
            ),
        )

    load_a = pltpu.make_async_copy(a_store, a_vm, local_sem.at[0])
    load_b = pltpu.make_async_copy(b_store, b_vm, local_sem.at[1])
    load_x = pltpu.make_async_copy(
        hidden.at[:, pl.ds(pl.multiple_of(me * depth, depth), depth)], xs.at[0], local_sem.at[2]
    )
    load_w = pltpu.make_async_copy(weight, w_vm, local_sem.at[3])
    load_a.start()
    load_x.start()
    load_b.start()
    load_w.start()

    barrier = pltpu.get_barrier_semaphore()
    for u in range(1, n_tp):
        pl.semaphore_signal(barrier, inc=1, device_id={"tp": flip(me, u, n_tp)})
    for u in range(1, n_serve):
        pl.semaphore_signal(barrier, inc=1, device_id={"serve": flip(group, u, n_serve)})
    pl.semaphore_wait(barrier, n_tp - 1 + n_serve - 1)

    for u in range(1, n_tp):
        x_copy(u).start()

    @pl.loop(0, n_serve)
    def _(u):
        d = flip(group, u, n_serve)

        def step(e, carry):
            count, chosen = carry[0], list(carry[1:])
            row = home[wanted[d, e]]
            hit = (row // held) == group
            slot = row % held
            for i in range(cap):
                chosen[i] = jnp.where(jnp.logical_and(hit, count == i), slot, chosen[i])
            return (count + jnp.where(hit, 1, 0), *chosen)

        result = lax.fori_loop(0, need, step, tuple(jnp.int32(0) for _ in range(cap + 1)))
        for i in range(cap):
            picks[u, i] = result[1 + i]

    load_a.wait()

    for u in range(n_serve - 1, 0, -1):
        for i in range(cap):
            send_a[u, i * rank:(i + 1) * rank, :] = a_vm[picks[u, i]]
        panel_copy(send_a, got_a, a_send, a_recv, u, u).start()

    load_b.wait()

    for u in range(n_serve - 1, 0, -1):
        for i in range(cap):
            send_b[u, i * rank:(i + 1) * rank, :] = b_vm[picks[u, i]]
        panel_copy(send_b, got_b, bs_send, bs_recv, u, u).start()

    for i in range(cap):
        send_a[0, i * rank:(i + 1) * rank, :] = a_vm[picks[0, i]]
        send_b[0, i * rank:(i + 1) * rank, :] = b_vm[picks[0, i]]

    @pl.loop(0, need)
    def _(e):
        owner = home[wanted[group, e]] // held

        def step(f, count):
            same = (home[wanted[group, f]] // held) == owner
            return count + jnp.where(jnp.logical_and(same, f < e), 1, 0)

        earlier = lax.fori_loop(0, need, step, jnp.int32(0))
        places[e] = flip(owner, group, n_serve) * cap + earlier

    per_block = tiles // n_tp
    for t in range(n_tp):
        j = flip(me, t, n_tp)

        @pl.loop(0, per_block)
        def _(k):
            place = places[tile_slot[j * per_block + k]]
            row_slot[t, pl.ds(pl.multiple_of(k * tile_rows, tile_rows), tile_rows), :] = jnp.full(
                (tile_rows, 128), place, jnp.int32
            )

    load_x.wait()
    load_w.wait()

    for t in range(n_tp):
        j = flip(me, t, n_tp)
        if t:
            x_copy(t).wait_recv()
        for u in range(1, n_tp):
            c = flip(me, u, n_tp)
            part = jnp.dot(
                xs[t], w_vm[:, pl.ds(pl.multiple_of(c * feats, feats), feats)],
                preferred_element_type=jnp.float32,
            )
            coded, scale = quantize(part)
            p_send[u, t] = coded
            p_scale_send[u, t] = scale
            for copy in part_copies(u, t):
                copy.start()

        own[t] = jnp.dot(
            xs[t], w_vm[:, pl.ds(pl.multiple_of(me * feats, feats), feats)],
            preferred_element_type=jnp.float32,
        )

    lane = lax.broadcasted_iota(jnp.int32, (rows, 128), 1)
    lane_half = lane // rank
    slots = row_slot[...].reshape(rows, 128)
    per = 128 // rank
    l_sum = jnp.zeros((rows, 128), jnp.float32)
    for u in range(n_serve):
        if u > 0:
            panel_copy(send_a, got_a, a_send, a_recv, u, u).wait_recv()
        found = lax.dot_general(
            xs[...].reshape(rows, depth), (got_a[u] if u else send_a[0]), (((1,), (1,)), ((), ())),
            preferred_element_type=jnp.float32,
        )
        for h in range(cap // per):
            keep = slots == u * cap + h * per + lane_half
            l_sum = l_sum + jnp.where(keep, found[:, h * 128:(h + 1) * 128], 0.0)
    l_sum = l_sum + pltpu.roll(l_sum, rank, 1)
    for t in range(n_tp):
        low_rows[flip(me, t, n_tp)] = l_sum[t * block:(t + 1) * block]
    l_sum = low_rows[...].reshape(rows, 128)
    left = lax.broadcasted_iota(jnp.int32, (half, 128), 1) < rank
    packed = jnp.where(left, l_sum[:half], l_sum[half:])
    coded, scale = quantize(packed)
    l_send[...] = coded
    l_scale_send[...] = scale
    for u in range(1, n_tp):
        for copy in low_copies(u):
            copy.start()
    total = packed
    for u in range(1, n_tp):
        for copy in low_copies(u):
            copy.wait_recv()
        total = total + restore(l_recv[u], l_scale_recv[u][0:1, :])
    turned = pltpu.roll(total, rank, 1)
    low_rows[...] = jnp.concatenate(
        [jnp.where(left, total, turned), jnp.where(left, turned, total)], axis=0
    ).reshape(n_tp, block, 128)
    low = jnp.concatenate([low_rows[flip(me, t, n_tp)] for t in range(n_tp)], axis=0)

    high = low.astype(jnp.bfloat16).astype(jnp.float32)
    rest = low - high
    update = jnp.zeros((rows, feats), jnp.float32)
    for u in range(n_serve):
        if u > 0:
            panel_copy(send_b, got_b, bs_send, bs_recv, u, u).wait_recv()
        for h in range(cap // per):
            keep = slots == u * cap + h * per + lane_half
            panel = (got_b if u else send_b)[u, h * 128:(h + 1) * 128, :]
            for piece in (high, rest):
                update = update + jnp.dot(
                    jnp.where(keep, piece, 0.0).astype(jnp.bfloat16), panel,
                    preferred_element_type=jnp.float32,
                )
    own[...] = own[...] + adapter_scale * update.reshape(n_tp, block, feats)

    for t in range(n_tp):
        j = flip(me, t, n_tp)
        result = own[t]
        for u in range(1, n_tp):
            for copy in part_copies(u, u ^ t):
                copy.wait_recv()
            result = result + restore(p_recv[u, u ^ t], p_scale_recv[u, u ^ t, 0:1, 0:1])
        out[pl.ds(pl.multiple_of(j * block, block), block), :] = result.astype(jnp.bfloat16)

    for u in range(1, n_tp):
        x_copy(u).wait_send()
        for copy in low_copies(u):
            copy.wait_send()

        for t in range(n_tp):
            for copy in part_copies(u, t):
                copy.wait_send()

    for u in range(1, n_serve):
        panel_copy(send_a, got_a, a_send, a_recv, u, u).wait_send()
        panel_copy(send_b, got_b, bs_send, bs_recv, u, u).wait_send()


def body(hidden, kv_weight, a_store, b_store, home, wanted, tile_slot):
    n_tp = lax.axis_size("tp")
    n_serve = lax.axis_size("serve")
    block, width = hidden.shape
    depth = width // n_tp
    held, _, rank = a_store.shape
    feats = b_store.shape[2]
    rows = block * n_tp
    cap = max(2, (wanted.shape[1] + n_serve - 1) // n_serve)
    cap = cap + cap % 2
    panels = jnp.transpose(a_store, (0, 2, 1))
    bf16, f32, i16 = jnp.bfloat16, jnp.float32, jnp.int16
    dma = pltpu.SemaphoreType.DMA
    smem = pl.BlockSpec(memory_space=pltpu.SMEM)
    hbm = pl.BlockSpec(memory_space=pl.ANY)
    scratch = [
        pltpu.VMEM((n_tp, block, depth), bf16),
        pltpu.VMEM(kv_weight.shape, bf16),
        pltpu.VMEM(panels.shape, bf16),
        pltpu.VMEM(b_store.shape, bf16),
        pltpu.VMEM((n_serve, cap * rank, depth), bf16),
        pltpu.VMEM((n_serve, cap * rank, feats), bf16),
        pltpu.VMEM((n_serve, cap * rank, depth), bf16),
        pltpu.VMEM((n_serve, cap * rank, feats), bf16),
        pltpu.VMEM((n_tp, n_tp, block, feats), i16),
        pltpu.VMEM((n_tp, n_tp, 8, 128), f32),
        pltpu.VMEM((n_tp, n_tp, block, feats), i16),
        pltpu.VMEM((n_tp, n_tp, 8, 128), f32),
        pltpu.VMEM((rows // 2, 128), i16),
        pltpu.VMEM((8, 128), f32),
        pltpu.VMEM((n_tp, rows // 2, 128), i16),
        pltpu.VMEM((n_tp, 8, 128), f32),
        pltpu.VMEM((n_tp, block, feats), f32),
        pltpu.VMEM((n_tp, block, 128), jnp.int32),
        pltpu.VMEM((n_tp, block, 128), f32),
        pltpu.SMEM((n_serve, cap), jnp.int32),
        pltpu.SMEM((wanted.shape[1],), jnp.int32),
        dma((4,)),
        dma((n_tp,)), dma((n_tp,)),
        dma((n_serve,)), dma((n_serve,)), dma((n_serve,)), dma((n_serve,)),
        dma((n_tp, n_tp)), dma((n_tp, n_tp)), dma((n_tp, n_tp)), dma((n_tp, n_tp)),
        dma((n_tp,)), dma((n_tp,)), dma((n_tp,)), dma((n_tp,)),
    ]
    return pl.pallas_call(
        functools.partial(kernel, (n_tp, n_serve, cap, held)),
        out_shape=jax.ShapeDtypeStruct((rows, feats), bf16),
        in_specs=[smem, smem, smem, hbm, hbm, hbm, hbm],
        out_specs=pl.BlockSpec(memory_space=pltpu.VMEM),
        scratch_shapes=scratch,
        compiler_params=pltpu.CompilerParams(
            collective_id=0, has_side_effects=True, vmem_limit_bytes=56 * 1024 * 1024
        ),
    )(home, wanted, tile_slot, hidden, kv_weight, panels, b_store)


def solution(mesh):
    in_specs = (
        P(("rep", "serve", "tp"), None),
        P("tp", None),
        P("serve", "tp", None),
        P("serve", None, "tp"),
        P("rep"),
        P("rep", None),
        P(("rep", "serve")),
    )
    out_specs = P(("rep", "serve"), "tp")
    return jax.shard_map(body, mesh=mesh, in_specs=in_specs, out_specs=out_specs, check_vma=False)
```

```python
import functools

import jax
import jax.numpy as jnp
from jax import lax
from jax.experimental import pallas as pl
from jax.experimental.pallas import tpu as pltpu
from jax.sharding import PartitionSpec as P

adapter_scale = 0.5
LEVELS = 32767.0


def flip(index, step, count):
    result, bit = 0, 1
    while bit < count:
        on = lax.rem(lax.div(index, jnp.int32(bit)), jnp.int32(2))
        if isinstance(step, int):
            turned = 1 - on if step & bit else on
        else:
            turned = lax.rem(on + lax.rem(lax.div(step, jnp.int32(bit)), jnp.int32(2)), jnp.int32(2))
        result = result + bit * turned
        bit *= 2
    return result


def quantize(values):
    top = jnp.maximum(jnp.max(jnp.abs(values)), 1e-30)
    coded = jnp.round(values * (LEVELS / top)).astype(jnp.int32).astype(jnp.int16)
    return coded, jnp.full((8, 128), top * (1.0 / LEVELS), jnp.float32)


def restore(coded, scale):
    return coded.astype(jnp.int32).astype(jnp.float32) * scale


def kernel(
    cfg,
    home, wanted, tile_slot, hidden, weight, a_store, b_store,
    out,
    xs, w_vm, a_vm, b_vm, send_a, send_b, got_a, got_b,
    p_send, p_scale_send, p_recv, p_scale_recv,
    l_send, l_scale_send, l_recv, l_scale_recv,
    own, row_slot, low_rows, picks, places,
    local_sem, x_send, x_recv, a_send, a_recv, bs_send, bs_recv,
    ps_send, ps_recv, psc_send, psc_recv,
    ls_send, ls_recv, lsc_send, lsc_recv,
):
    n_tp, n_serve, cap, held = cfg
    need = wanted.shape[1]
    tiles = tile_slot.shape[0]
    block, depth = xs.shape[1], xs.shape[2]
    rows = n_tp * block
    tile_rows = rows // tiles
    rank = a_vm.shape[1]
    feats = out.shape[1]
    half = rows // 2
    me = lax.axis_index("tp")
    group = lax.axis_index("serve")

    def x_copy(u):
        j = flip(me, u, n_tp)
        return pltpu.make_async_remote_copy(
            src_ref=hidden.at[:, pl.ds(pl.multiple_of(j * depth, depth), depth)],
            dst_ref=xs.at[u],
            send_sem=x_send.at[u], recv_sem=x_recv.at[u],
            device_id={"tp": j},
        )

    def panel_copy(src, dst, ssem, rsem, u, landing):
        d = flip(group, u, n_serve)
        return pltpu.make_async_remote_copy(
            src_ref=src.at[u], dst_ref=dst.at[landing],
            send_sem=ssem.at[u], recv_sem=rsem.at[u],
            device_id={"serve": d},
        )

    def part_copies(u, t):
        c = flip(me, u & -u, n_tp)
        return (
            pltpu.make_async_remote_copy(
                src_ref=p_send.at[u, t], dst_ref=p_recv.at[u, t],
                send_sem=ps_send.at[u, t], recv_sem=ps_recv.at[u, t],
                device_id={"tp": c},
            ),
            pltpu.make_async_remote_copy(
                src_ref=p_scale_send.at[u, t], dst_ref=p_scale_recv.at[u, t],
                send_sem=psc_send.at[u, t], recv_sem=psc_recv.at[u, t],
                device_id={"tp": c},
            ),
        )

    def low_copies(u):
        c = flip(me, u, n_tp)
        return (
            pltpu.make_async_remote_copy(
                src_ref=l_send, dst_ref=l_recv.at[u],
                send_sem=ls_send.at[u], recv_sem=ls_recv.at[u],
                device_id={"tp": c},
            ),
            pltpu.make_async_remote_copy(
                src_ref=l_scale_send, dst_ref=l_scale_recv.at[u],
                send_sem=lsc_send.at[u], recv_sem=lsc_recv.at[u],
                device_id={"tp": c},
            ),
        )

    load_a = pltpu.make_async_copy(a_store, a_vm, local_sem.at[0])
    load_b = pltpu.make_async_copy(b_store, b_vm, local_sem.at[1])
    load_x = pltpu.make_async_copy(
        hidden.at[:, pl.ds(pl.multiple_of(me * depth, depth), depth)], xs.at[0], local_sem.at[2]
    )
    load_w = pltpu.make_async_copy(weight, w_vm, local_sem.at[3])
    load_a.start()
    load_x.start()
    load_b.start()
    load_w.start()

    barrier = pltpu.get_barrier_semaphore()
    for u in range(1, n_tp):
        pl.semaphore_signal(barrier, inc=1, device_id={"tp": flip(me, u, n_tp)})
    for u in range(1, n_serve):
        pl.semaphore_signal(barrier, inc=1, device_id={"serve": flip(group, u, n_serve)})
    pl.semaphore_wait(barrier, n_tp - 1 + n_serve - 1)

    for u in range(1, n_tp):
        x_copy(u).start()

    @pl.loop(0, n_serve)
    def _(u):
        d = flip(group, u, n_serve)

        def step(e, carry):
            count, chosen = carry[0], list(carry[1:])
            row = home[wanted[d, e]]
            hit = (row // held) == group
            slot = row % held
            for i in range(cap):
                chosen[i] = jnp.where(jnp.logical_and(hit, count == i), slot, chosen[i])
            return (count + jnp.where(hit, 1, 0), *chosen)

        result = lax.fori_loop(0, need, step, tuple(jnp.int32(0) for _ in range(cap + 1)))
        for i in range(cap):
            picks[u, i] = result[1 + i]

    load_a.wait()

    for u in range(n_serve - 1, 0, -1):
        for i in range(cap):
            send_a[u, i * rank:(i + 1) * rank, :] = a_vm[picks[u, i]]
        panel_copy(send_a, got_a, a_send, a_recv, u, u).start()

    load_b.wait()

    for u in range(n_serve - 1, 0, -1):
        for i in range(cap):
            send_b[u, i * rank:(i + 1) * rank, :] = b_vm[picks[u, i]]
        panel_copy(send_b, got_b, bs_send, bs_recv, u, u).start()

    for i in range(cap):
        send_a[0, i * rank:(i + 1) * rank, :] = a_vm[picks[0, i]]
        send_b[0, i * rank:(i + 1) * rank, :] = b_vm[picks[0, i]]

    @pl.loop(0, need)
    def _(e):
        owner = home[wanted[group, e]] // held

        def step(f, count):
            same = (home[wanted[group, f]] // held) == owner
            return count + jnp.where(jnp.logical_and(same, f < e), 1, 0)

        earlier = lax.fori_loop(0, need, step, jnp.int32(0))
        places[e] = flip(owner, group, n_serve) * cap + earlier

    per_block = tiles // n_tp
    for t in range(n_tp):
        j = flip(me, t, n_tp)

        @pl.loop(0, per_block)
        def _(k):
            place = places[tile_slot[j * per_block + k]]
            row_slot[t, pl.ds(pl.multiple_of(k * tile_rows, tile_rows), tile_rows), :] = jnp.full(
                (tile_rows, 128), place, jnp.int32
            )

    load_x.wait()
    load_w.wait()

    def product(t, u):
        c = flip(me, u, n_tp)
        return jnp.dot(
            xs[t], w_vm[:, pl.ds(pl.multiple_of(c * feats, feats), feats)],
            preferred_element_type=jnp.float32,
        )

    def send_part(u, t, part):
        coded, scale = quantize(part)
        p_send[u, t] = coded
        p_scale_send[u, t] = scale
        for copy in part_copies(u, t):
            copy.start()

    def with_received(u, t):
        total = own[u // 2, t]
        bit = 1
        while bit < ((u & -u) or n_tp):
            v, q = u | bit, t ^ bit
            for copy in part_copies(v, q):
                copy.wait_recv()
            total = total + restore(p_recv[v, q], p_scale_recv[v, q, 0:1, 0:1])
            bit *= 2
        return total

    def forward(bit, places_of):
        for t in places_of:
            for u in range(bit, n_tp, 2 * bit):
                send_part(u, t, with_received(u, t))

    for t in range(n_tp):
        if t:
            x_copy(t).wait_recv()
        for u in range(1, n_tp, 2):
            send_part(u, t, product(t, u))
        for u in range(0, n_tp, 2):
            own[u // 2, t] = product(t, u)
        if t >= 2 and t % 2 == 0:
            forward(2, (t - 2, t - 1))
    forward(2, (n_tp - 2, n_tp - 1))
    bit = 4
    while bit < n_tp:
        forward(bit, range(n_tp))
        bit *= 2

    lane = lax.broadcasted_iota(jnp.int32, (rows, 128), 1)
    lane_half = lane // rank
    slots = row_slot[...].reshape(rows, 128)
    per = 128 // rank
    l_sum = jnp.zeros((rows, 128), jnp.float32)
    for u in range(n_serve):
        if u > 0:
            panel_copy(send_a, got_a, a_send, a_recv, u, u).wait_recv()
        found = lax.dot_general(
            xs[...].reshape(rows, depth), (got_a[u] if u else send_a[0]), (((1,), (1,)), ((), ())),
            preferred_element_type=jnp.float32,
        )
        for h in range(cap // per):
            keep = slots == u * cap + h * per + lane_half
            l_sum = l_sum + jnp.where(keep, found[:, h * 128:(h + 1) * 128], 0.0)
    l_sum = l_sum + pltpu.roll(l_sum, rank, 1)
    for t in range(n_tp):
        low_rows[flip(me, t, n_tp)] = l_sum[t * block:(t + 1) * block]
    l_sum = low_rows[...].reshape(rows, 128)
    left = lax.broadcasted_iota(jnp.int32, (half, 128), 1) < rank
    packed = jnp.where(left, l_sum[:half], l_sum[half:])
    coded, scale = quantize(packed)
    l_send[...] = coded
    l_scale_send[...] = scale
    for u in range(1, n_tp):
        for copy in low_copies(u):
            copy.start()
    total = packed
    for u in range(1, n_tp):
        for copy in low_copies(u):
            copy.wait_recv()
        total = total + restore(l_recv[u], l_scale_recv[u][0:1, :])
    turned = pltpu.roll(total, rank, 1)
    low_rows[...] = jnp.concatenate(
        [jnp.where(left, total, turned), jnp.where(left, turned, total)], axis=0
    ).reshape(n_tp, block, 128)
    low = jnp.concatenate([low_rows[flip(me, t, n_tp)] for t in range(n_tp)], axis=0)

    high = low.astype(jnp.bfloat16).astype(jnp.float32)
    rest = low - high
    update = jnp.zeros((rows, feats), jnp.float32)
    for u in range(n_serve):
        if u > 0:
            panel_copy(send_b, got_b, bs_send, bs_recv, u, u).wait_recv()
        for h in range(cap // per):
            keep = slots == u * cap + h * per + lane_half
            panel = (got_b if u else send_b)[u, h * 128:(h + 1) * 128, :]
            for piece in (high, rest):
                update = update + jnp.dot(
                    jnp.where(keep, piece, 0.0).astype(jnp.bfloat16), panel,
                    preferred_element_type=jnp.float32,
                )
    own[0] = own[0] + adapter_scale * update.reshape(n_tp, block, feats)

    for t in range(n_tp):
        j = flip(me, t, n_tp)
        result = with_received(0, t)
        out[pl.ds(pl.multiple_of(j * block, block), block), :] = result.astype(jnp.bfloat16)

    for u in range(1, n_tp):
        x_copy(u).wait_send()
        for copy in low_copies(u):
            copy.wait_send()

        for t in range(n_tp):
            for copy in part_copies(u, t):
                copy.wait_send()

    for u in range(1, n_serve):
        panel_copy(send_a, got_a, a_send, a_recv, u, u).wait_send()
        panel_copy(send_b, got_b, bs_send, bs_recv, u, u).wait_send()


def body(hidden, kv_weight, a_store, b_store, home, wanted, tile_slot):
    n_tp = lax.axis_size("tp")
    n_serve = lax.axis_size("serve")
    block, width = hidden.shape
    depth = width // n_tp
    held, _, rank = a_store.shape
    feats = b_store.shape[2]
    rows = block * n_tp
    cap = max(2, (wanted.shape[1] + n_serve - 1) // n_serve)
    cap = cap + cap % 2
    panels = jnp.transpose(a_store, (0, 2, 1))
    bf16, f32, i16 = jnp.bfloat16, jnp.float32, jnp.int16
    dma = pltpu.SemaphoreType.DMA
    smem = pl.BlockSpec(memory_space=pltpu.SMEM)
    hbm = pl.BlockSpec(memory_space=pl.ANY)
    scratch = [
        pltpu.VMEM((n_tp, block, depth), bf16),
        pltpu.VMEM(kv_weight.shape, bf16),
        pltpu.VMEM(panels.shape, bf16),
        pltpu.VMEM(b_store.shape, bf16),
        pltpu.VMEM((n_serve, cap * rank, depth), bf16),
        pltpu.VMEM((n_serve, cap * rank, feats), bf16),
        pltpu.VMEM((n_serve, cap * rank, depth), bf16),
        pltpu.VMEM((n_serve, cap * rank, feats), bf16),
        pltpu.VMEM((n_tp, n_tp, block, feats), i16),
        pltpu.VMEM((n_tp, n_tp, 8, 128), f32),
        pltpu.VMEM((n_tp, n_tp, block, feats), i16),
        pltpu.VMEM((n_tp, n_tp, 8, 128), f32),
        pltpu.VMEM((rows // 2, 128), i16),
        pltpu.VMEM((8, 128), f32),
        pltpu.VMEM((n_tp, rows // 2, 128), i16),
        pltpu.VMEM((n_tp, 8, 128), f32),
        pltpu.VMEM((n_tp // 2, n_tp, block, feats), f32),
        pltpu.VMEM((n_tp, block, 128), jnp.int32),
        pltpu.VMEM((n_tp, block, 128), f32),
        pltpu.SMEM((n_serve, cap), jnp.int32),
        pltpu.SMEM((wanted.shape[1],), jnp.int32),
        dma((4,)),
        dma((n_tp,)), dma((n_tp,)),
        dma((n_serve,)), dma((n_serve,)), dma((n_serve,)), dma((n_serve,)),
        dma((n_tp, n_tp)), dma((n_tp, n_tp)), dma((n_tp, n_tp)), dma((n_tp, n_tp)),
        dma((n_tp,)), dma((n_tp,)), dma((n_tp,)), dma((n_tp,)),
    ]
    return pl.pallas_call(
        functools.partial(kernel, (n_tp, n_serve, cap, held)),
        out_shape=jax.ShapeDtypeStruct((rows, feats), bf16),
        in_specs=[smem, smem, smem, hbm, hbm, hbm, hbm],
        out_specs=pl.BlockSpec(memory_space=pltpu.VMEM),
        scratch_shapes=scratch,
        compiler_params=pltpu.CompilerParams(
            collective_id=0, has_side_effects=True, vmem_limit_bytes=56 * 1024 * 1024
        ),
    )(home, wanted, tile_slot, hidden, kv_weight, panels, b_store)


def solution(mesh):
    in_specs = (
        P(("rep", "serve", "tp"), None),
        P("tp", None),
        P("serve", "tp", None),
        P("serve", None, "tp"),
        P("rep"),
        P("rep", None),
        P(("rep", "serve")),
    )
    out_specs = P(("rep", "serve"), "tp")
    return jax.shard_map(body, mesh=mesh, in_specs=in_specs, out_specs=out_specs, check_vma=False)
```

```python
import functools

import jax
import jax.numpy as jnp
from jax import lax
from jax.experimental import pallas as pl
from jax.experimental.pallas import tpu as pltpu
from jax.sharding import PartitionSpec as P

adapter_scale = 0.5
LEVELS = 32767.0


def flip(index, step, count):
    result, bit = 0, 1
    while bit < count:
        on = lax.rem(lax.div(index, jnp.int32(bit)), jnp.int32(2))
        if isinstance(step, int):
            turned = 1 - on if step & bit else on
        else:
            turned = lax.rem(on + lax.rem(lax.div(step, jnp.int32(bit)), jnp.int32(2)), jnp.int32(2))
        result = result + bit * turned
        bit *= 2
    return result


def quantize(values):
    top = jnp.maximum(jnp.max(jnp.abs(values)), 1e-30)
    coded = jnp.round(values * (LEVELS / top)).astype(jnp.int32).astype(jnp.int16)
    return coded, jnp.full((8, 128), top * (1.0 / LEVELS), jnp.float32)


def restore(coded, scale):
    return coded.astype(jnp.int32).astype(jnp.float32) * scale


def kernel(
    cfg,
    home, wanted, tile_slot, hidden, weight, a_store, b_store,
    out,
    xs, w_vm, a_vm, b_vm, send_a, send_b, got_a, got_b,
    p_send, p_scale_send, p_recv, p_scale_recv,
    l_send, l_scale_send, l_recv, l_scale_recv,
    own, row_slot, low_rows, picks, places,
    local_sem, x_send, x_recv, a_send, a_recv, bs_send, bs_recv,
    ps_send, ps_recv, psc_send, psc_recv,
    ls_send, ls_recv, lsc_send, lsc_recv,
):
    n_tp, n_serve, cap, held = cfg
    need = wanted.shape[1]
    tiles = tile_slot.shape[0]
    block, depth = xs.shape[1], xs.shape[2]
    rows = n_tp * block
    tile_rows = rows // tiles
    rank = a_vm.shape[1]
    feats = out.shape[1]
    half = rows // 2
    me = lax.axis_index("tp")
    group = lax.axis_index("serve")

    def x_copy(u):
        j = flip(me, u, n_tp)
        return pltpu.make_async_remote_copy(
            src_ref=hidden.at[:, pl.ds(pl.multiple_of(j * depth, depth), depth)],
            dst_ref=xs.at[u],
            send_sem=x_send.at[u], recv_sem=x_recv.at[u],
            device_id={"tp": j},
        )

    def panel_copy(src, dst, ssem, rsem, u, landing):
        d = flip(group, u, n_serve)
        return pltpu.make_async_remote_copy(
            src_ref=src.at[u], dst_ref=dst.at[landing],
            send_sem=ssem.at[u], recv_sem=rsem.at[u],
            device_id={"serve": d},
        )

    def part_copies(u, t):
        c = flip(me, u & -u, n_tp)
        return (
            pltpu.make_async_remote_copy(
                src_ref=p_send.at[u, t], dst_ref=p_recv.at[u, t],
                send_sem=ps_send.at[u, t], recv_sem=ps_recv.at[u, t],
                device_id={"tp": c},
            ),
            pltpu.make_async_remote_copy(
                src_ref=p_scale_send.at[u, t], dst_ref=p_scale_recv.at[u, t],
                send_sem=psc_send.at[u, t], recv_sem=psc_recv.at[u, t],
                device_id={"tp": c},
            ),
        )

    def low_copies(u):
        c = flip(me, u, n_tp)
        return (
            pltpu.make_async_remote_copy(
                src_ref=l_send, dst_ref=l_recv.at[u],
                send_sem=ls_send.at[u], recv_sem=ls_recv.at[u],
                device_id={"tp": c},
            ),
            pltpu.make_async_remote_copy(
                src_ref=l_scale_send, dst_ref=l_scale_recv.at[u],
                send_sem=lsc_send.at[u], recv_sem=lsc_recv.at[u],
                device_id={"tp": c},
            ),
        )

    load_a = pltpu.make_async_copy(a_store, a_vm, local_sem.at[0])
    load_b = pltpu.make_async_copy(b_store, b_vm, local_sem.at[1])
    load_x = pltpu.make_async_copy(
        hidden.at[:, pl.ds(pl.multiple_of(me * depth, depth), depth)], xs.at[0], local_sem.at[2]
    )
    load_w = pltpu.make_async_copy(weight, w_vm, local_sem.at[3])
    load_a.start()
    load_x.start()
    load_w.start()
    load_b.start()

    barrier = pltpu.get_barrier_semaphore()
    for u in range(1, n_tp):
        pl.semaphore_signal(barrier, inc=1, device_id={"tp": flip(me, u, n_tp)})
    for u in range(1, n_serve):
        pl.semaphore_signal(barrier, inc=1, device_id={"serve": flip(group, u, n_serve)})
    pl.semaphore_wait(barrier, n_tp - 1 + n_serve - 1)

    for u in range(1, n_tp):
        x_copy(u).start()

    @pl.loop(0, n_serve)
    def _(u):
        d = flip(group, u, n_serve)

        def step(e, carry):
            count, chosen = carry[0], list(carry[1:])
            row = home[wanted[d, e]]
            hit = (row // held) == group
            slot = row % held
            for i in range(cap):
                chosen[i] = jnp.where(jnp.logical_and(hit, count == i), slot, chosen[i])
            return (count + jnp.where(hit, 1, 0), *chosen)

        result = lax.fori_loop(0, need, step, tuple(jnp.int32(0) for _ in range(cap + 1)))
        for i in range(cap):
            picks[u, i] = result[1 + i]

    load_a.wait()

    for u in range(n_serve - 1, 0, -1):
        for i in range(cap):
            send_a[u, i * rank:(i + 1) * rank, :] = a_vm[picks[u, i]]
        panel_copy(send_a, got_a, a_send, a_recv, u, u).start()

    for i in range(cap):
        send_a[0, i * rank:(i + 1) * rank, :] = a_vm[picks[0, i]]

    load_x.wait()
    load_w.wait()

    def place_rows():
        load_b.wait()

        for u in range(n_serve - 1, 0, -1):
            for i in range(cap):
                send_b[u, i * rank:(i + 1) * rank, :] = b_vm[picks[u, i]]
            panel_copy(send_b, got_b, bs_send, bs_recv, u, u).start()

        for i in range(cap):
            send_b[0, i * rank:(i + 1) * rank, :] = b_vm[picks[0, i]]

        @pl.loop(0, need)
        def _(e):
            owner = home[wanted[group, e]] // held

            def step(f, count):
                same = (home[wanted[group, f]] // held) == owner
                return count + jnp.where(jnp.logical_and(same, f < e), 1, 0)

            earlier = lax.fori_loop(0, need, step, jnp.int32(0))
            places[e] = flip(owner, group, n_serve) * cap + earlier

        per_block = tiles // n_tp
        for t in range(n_tp):
            j = flip(me, t, n_tp)

            @pl.loop(0, per_block)
            def _(k):
                place = places[tile_slot[j * per_block + k]]
                row_slot[t, pl.ds(pl.multiple_of(k * tile_rows, tile_rows), tile_rows), :] = jnp.full(
                    (tile_rows, 128), place, jnp.int32
                )


    def product(t, u):
        c = flip(me, u, n_tp)
        return jnp.dot(
            xs[t], w_vm[:, pl.ds(pl.multiple_of(c * feats, feats), feats)],
            preferred_element_type=jnp.float32,
        )

    def send_part(u, t, part):
        coded, scale = quantize(part)
        p_send[u, t] = coded
        p_scale_send[u, t] = scale
        for copy in part_copies(u, t):
            copy.start()

    def with_received(u, t):
        total = own[u // 2, t]
        bit = 1
        while bit < ((u & -u) or n_tp):
            v, q = u | bit, t ^ bit
            for copy in part_copies(v, q):
                copy.wait_recv()
            total = total + restore(p_recv[v, q], p_scale_recv[v, q, 0:1, 0:1])
            bit *= 2
        return total

    def forward(bit, places_of):
        for t in places_of:
            for u in range(bit, n_tp, 2 * bit):
                send_part(u, t, with_received(u, t))

    for t in range(n_tp):
        if t:
            x_copy(t).wait_recv()
        for u in range(1, n_tp, 2):
            send_part(u, t, product(t, u))
        for u in range(0, n_tp, 2):
            own[u // 2, t] = product(t, u)
        if t == 1:
            place_rows()
        if t >= 2 and t % 2 == 0:
            forward(2, (t - 2, t - 1))
    forward(2, (n_tp - 2, n_tp - 1))
    bit = 4
    while bit < n_tp:
        forward(bit, range(n_tp))
        bit *= 2

    lane = lax.broadcasted_iota(jnp.int32, (rows, 128), 1)
    lane_half = lane // rank
    slots = row_slot[...].reshape(rows, 128)
    per = 128 // rank
    l_sum = jnp.zeros((rows, 128), jnp.float32)
    for u in range(n_serve):
        if u > 0:
            panel_copy(send_a, got_a, a_send, a_recv, u, u).wait_recv()
        found = lax.dot_general(
            xs[...].reshape(rows, depth), (got_a[u] if u else send_a[0]), (((1,), (1,)), ((), ())),
            preferred_element_type=jnp.float32,
        )
        for h in range(cap // per):
            keep = slots == u * cap + h * per + lane_half
            l_sum = l_sum + jnp.where(keep, found[:, h * 128:(h + 1) * 128], 0.0)
    l_sum = l_sum + pltpu.roll(l_sum, rank, 1)
    for t in range(n_tp):
        low_rows[flip(me, t, n_tp)] = l_sum[t * block:(t + 1) * block]
    l_sum = low_rows[...].reshape(rows, 128)
    left = lax.broadcasted_iota(jnp.int32, (half, 128), 1) < rank
    packed = jnp.where(left, l_sum[:half], l_sum[half:])
    coded, scale = quantize(packed)
    l_send[...] = coded
    l_scale_send[...] = scale
    for u in range(1, n_tp):
        for copy in low_copies(u):
            copy.start()
    total = packed
    for u in range(1, n_tp):
        for copy in low_copies(u):
            copy.wait_recv()
        total = total + restore(l_recv[u], l_scale_recv[u][0:1, :])
    turned = pltpu.roll(total, rank, 1)
    low_rows[...] = jnp.concatenate(
        [jnp.where(left, total, turned), jnp.where(left, turned, total)], axis=0
    ).reshape(n_tp, block, 128)
    low = jnp.concatenate([low_rows[flip(me, t, n_tp)] for t in range(n_tp)], axis=0)

    high = low.astype(jnp.bfloat16).astype(jnp.float32)
    rest = low - high
    update = jnp.zeros((rows, feats), jnp.float32)
    for u in range(n_serve):
        if u > 0:
            panel_copy(send_b, got_b, bs_send, bs_recv, u, u).wait_recv()
        for h in range(cap // per):
            keep = slots == u * cap + h * per + lane_half
            panel = (got_b if u else send_b)[u, h * 128:(h + 1) * 128, :]
            for piece in (high, rest):
                update = update + jnp.dot(
                    jnp.where(keep, piece, 0.0).astype(jnp.bfloat16), panel,
                    preferred_element_type=jnp.float32,
                )
    own[0] = own[0] + adapter_scale * update.reshape(n_tp, block, feats)

    for t in range(n_tp):
        j = flip(me, t, n_tp)
        result = with_received(0, t)
        out[pl.ds(pl.multiple_of(j * block, block), block), :] = result.astype(jnp.bfloat16)

    for u in range(1, n_tp):
        x_copy(u).wait_send()
        for copy in low_copies(u):
            copy.wait_send()

        for t in range(n_tp):
            for copy in part_copies(u, t):
                copy.wait_send()

    for u in range(1, n_serve):
        panel_copy(send_a, got_a, a_send, a_recv, u, u).wait_send()
        panel_copy(send_b, got_b, bs_send, bs_recv, u, u).wait_send()


def body(hidden, kv_weight, a_store, b_store, home, wanted, tile_slot):
    n_tp = lax.axis_size("tp")
    n_serve = lax.axis_size("serve")
    block, width = hidden.shape
    depth = width // n_tp
    held, _, rank = a_store.shape
    feats = b_store.shape[2]
    rows = block * n_tp
    cap = max(2, (wanted.shape[1] + n_serve - 1) // n_serve)
    cap = cap + cap % 2
    panels = jnp.transpose(a_store, (0, 2, 1))
    bf16, f32, i16 = jnp.bfloat16, jnp.float32, jnp.int16
    dma = pltpu.SemaphoreType.DMA
    smem = pl.BlockSpec(memory_space=pltpu.SMEM)
    hbm = pl.BlockSpec(memory_space=pl.ANY)
    scratch = [
        pltpu.VMEM((n_tp, block, depth), bf16),
        pltpu.VMEM(kv_weight.shape, bf16),
        pltpu.VMEM(panels.shape, bf16),
        pltpu.VMEM(b_store.shape, bf16),
        pltpu.VMEM((n_serve, cap * rank, depth), bf16),
        pltpu.VMEM((n_serve, cap * rank, feats), bf16),
        pltpu.VMEM((n_serve, cap * rank, depth), bf16),
        pltpu.VMEM((n_serve, cap * rank, feats), bf16),
        pltpu.VMEM((n_tp, n_tp, block, feats), i16),
        pltpu.VMEM((n_tp, n_tp, 8, 128), f32),
        pltpu.VMEM((n_tp, n_tp, block, feats), i16),
        pltpu.VMEM((n_tp, n_tp, 8, 128), f32),
        pltpu.VMEM((rows // 2, 128), i16),
        pltpu.VMEM((8, 128), f32),
        pltpu.VMEM((n_tp, rows // 2, 128), i16),
        pltpu.VMEM((n_tp, 8, 128), f32),
        pltpu.VMEM((n_tp // 2, n_tp, block, feats), f32),
        pltpu.VMEM((n_tp, block, 128), jnp.int32),
        pltpu.VMEM((n_tp, block, 128), f32),
        pltpu.SMEM((n_serve, cap), jnp.int32),
        pltpu.SMEM((wanted.shape[1],), jnp.int32),
        dma((4,)),
        dma((n_tp,)), dma((n_tp,)),
        dma((n_serve,)), dma((n_serve,)), dma((n_serve,)), dma((n_serve,)),
        dma((n_tp, n_tp)), dma((n_tp, n_tp)), dma((n_tp, n_tp)), dma((n_tp, n_tp)),
        dma((n_tp,)), dma((n_tp,)), dma((n_tp,)), dma((n_tp,)),
    ]
    return pl.pallas_call(
        functools.partial(kernel, (n_tp, n_serve, cap, held)),
        out_shape=jax.ShapeDtypeStruct((rows, feats), bf16),
        in_specs=[smem, smem, smem, hbm, hbm, hbm, hbm],
        out_specs=pl.BlockSpec(memory_space=pltpu.VMEM),
        scratch_shapes=scratch,
        compiler_params=pltpu.CompilerParams(
            collective_id=0, has_side_effects=True, vmem_limit_bytes=56 * 1024 * 1024
        ),
    )(home, wanted, tile_slot, hidden, kv_weight, panels, b_store)


def solution(mesh):
    in_specs = (
        P(("rep", "serve", "tp"), None),
        P("tp", None),
        P("serve", "tp", None),
        P("serve", None, "tp"),
        P("rep"),
        P("rep", None),
        P(("rep", "serve")),
    )
    out_specs = P(("rep", "serve"), "tp")
    return jax.shard_map(body, mesh=mesh, in_specs=in_specs, out_specs=out_specs, check_vma=False)
```

```python
import functools

import jax
import jax.numpy as jnp
from jax import lax
from jax.experimental import pallas as pl
from jax.experimental.pallas import tpu as pltpu
from jax.sharding import PartitionSpec as P

adapter_scale = 0.5
LEVELS = 32767.0


def flip(index, step, count):
    result, bit = 0, 1
    while bit < count:
        on = lax.rem(lax.div(index, jnp.int32(bit)), jnp.int32(2))
        if isinstance(step, int):
            turned = 1 - on if step & bit else on
        else:
            turned = lax.rem(on + lax.rem(lax.div(step, jnp.int32(bit)), jnp.int32(2)), jnp.int32(2))
        result = result + bit * turned
        bit *= 2
    return result


def quantize(values):
    top = jnp.maximum(jnp.max(jnp.abs(values)), 1e-30)
    coded = jnp.round(values * (LEVELS / top)).astype(jnp.int32).astype(jnp.int16)
    return coded, jnp.full((8, 128), top * (1.0 / LEVELS), jnp.float32)


def restore(coded, scale):
    return coded.astype(jnp.int32).astype(jnp.float32) * scale


def kernel(
    cfg,
    home, wanted, tile_slot, hidden, weight, a_store, b_store,
    out,
    xs, w_vm, a_vm, b_vm, send_a, send_b, got_a, got_b,
    p_send, p_scale_send, p_recv, p_scale_recv,
    l_send, l_scale_send, l_recv, l_scale_recv,
    own, row_slot, low_rows, picks, places,
    local_sem, x_send, x_recv, a_send, a_recv, bs_send, bs_recv,
    ps_send, ps_recv, psc_send, psc_recv,
    ls_send, ls_recv, lsc_send, lsc_recv,
):
    n_tp, n_serve, cap, held = cfg
    need = wanted.shape[1]
    tiles = tile_slot.shape[0]
    block, depth = xs.shape[1], xs.shape[2]
    rows = n_tp * block
    tile_rows = rows // tiles
    rank = a_vm.shape[1]
    feats = out.shape[1]
    half = rows // 2
    me = lax.axis_index("tp")
    group = lax.axis_index("serve")

    def x_copy(u):
        j = flip(me, u, n_tp)
        return pltpu.make_async_remote_copy(
            src_ref=hidden.at[:, pl.ds(pl.multiple_of(j * depth, depth), depth)],
            dst_ref=xs.at[u],
            send_sem=x_send.at[u], recv_sem=x_recv.at[u],
            device_id={"tp": j},
        )

    def panel_copy(src, dst, ssem, rsem, u, landing):
        d = flip(group, u, n_serve)
        return pltpu.make_async_remote_copy(
            src_ref=src.at[u], dst_ref=dst.at[landing],
            send_sem=ssem.at[u], recv_sem=rsem.at[u],
            device_id={"serve": d},
        )

    def part_copies(u, t):
        c = flip(me, u & -u, n_tp)
        return (
            pltpu.make_async_remote_copy(
                src_ref=p_send.at[u, t], dst_ref=p_recv.at[u, t],
                send_sem=ps_send.at[u, t], recv_sem=ps_recv.at[u, t],
                device_id={"tp": c},
            ),
            pltpu.make_async_remote_copy(
                src_ref=p_scale_send.at[u, t], dst_ref=p_scale_recv.at[u, t],
                send_sem=psc_send.at[u, t], recv_sem=psc_recv.at[u, t],
                device_id={"tp": c},
            ),
        )

    def low_copies(u):
        c = flip(me, u, n_tp)
        return (
            pltpu.make_async_remote_copy(
                src_ref=l_send, dst_ref=l_recv.at[u],
                send_sem=ls_send.at[u], recv_sem=ls_recv.at[u],
                device_id={"tp": c},
            ),
            pltpu.make_async_remote_copy(
                src_ref=l_scale_send, dst_ref=l_scale_recv.at[u],
                send_sem=lsc_send.at[u], recv_sem=lsc_recv.at[u],
                device_id={"tp": c},
            ),
        )

    load_a = pltpu.make_async_copy(a_store, a_vm, local_sem.at[0])
    load_b = pltpu.make_async_copy(b_store, b_vm, local_sem.at[1])
    load_x = pltpu.make_async_copy(
        hidden.at[:, pl.ds(pl.multiple_of(me * depth, depth), depth)], xs.at[0], local_sem.at[2]
    )
    load_w = pltpu.make_async_copy(weight, w_vm, local_sem.at[3])
    load_a.start()
    load_x.start()
    load_w.start()
    load_b.start()

    barrier = pltpu.get_barrier_semaphore()
    for u in range(1, n_tp):
        pl.semaphore_signal(barrier, inc=1, device_id={"tp": flip(me, u, n_tp)})
    for u in range(1, n_serve):
        pl.semaphore_signal(barrier, inc=1, device_id={"serve": flip(group, u, n_serve)})
    pl.semaphore_wait(barrier, n_tp - 1 + n_serve - 1)

    for u in range(n_tp - 1, 0, -1):
        x_copy(u).start()

    @pl.loop(0, n_serve)
    def _(u):
        d = flip(group, u, n_serve)

        def step(e, carry):
            count, chosen = carry[0], list(carry[1:])
            row = home[wanted[d, e]]
            hit = (row // held) == group
            slot = row % held
            for i in range(cap):
                chosen[i] = jnp.where(jnp.logical_and(hit, count == i), slot, chosen[i])
            return (count + jnp.where(hit, 1, 0), *chosen)

        result = lax.fori_loop(0, need, step, tuple(jnp.int32(0) for _ in range(cap + 1)))
        for i in range(cap):
            picks[u, i] = result[1 + i]

    load_a.wait()

    for u in range(n_serve - 1, 0, -1):
        for i in range(cap):
            send_a[u, i * rank:(i + 1) * rank, :] = a_vm[picks[u, i]]
        panel_copy(send_a, got_a, a_send, a_recv, u, u).start()

    for i in range(cap):
        send_a[0, i * rank:(i + 1) * rank, :] = a_vm[picks[0, i]]

    load_x.wait()
    load_w.wait()

    def place_rows():
        load_b.wait()

        for u in range(n_serve - 1, 0, -1):
            for i in range(cap):
                send_b[u, i * rank:(i + 1) * rank, :] = b_vm[picks[u, i]]
            panel_copy(send_b, got_b, bs_send, bs_recv, u, u).start()

        for i in range(cap):
            send_b[0, i * rank:(i + 1) * rank, :] = b_vm[picks[0, i]]

        @pl.loop(0, need)
        def _(e):
            owner = home[wanted[group, e]] // held

            def step(f, count):
                same = (home[wanted[group, f]] // held) == owner
                return count + jnp.where(jnp.logical_and(same, f < e), 1, 0)

            earlier = lax.fori_loop(0, need, step, jnp.int32(0))
            places[e] = flip(owner, group, n_serve) * cap + earlier

        per_block = tiles // n_tp
        for t in range(n_tp):
            j = flip(me, t, n_tp)

            @pl.loop(0, per_block)
            def _(k):
                place = places[tile_slot[j * per_block + k]]
                row_slot[t, pl.ds(pl.multiple_of(k * tile_rows, tile_rows), tile_rows), :] = jnp.full(
                    (tile_rows, 128), place, jnp.int32
                )


    def product(t, u):
        c = flip(me, u, n_tp)
        return jnp.dot(
            xs[t], w_vm[:, pl.ds(pl.multiple_of(c * feats, feats), feats)],
            preferred_element_type=jnp.float32,
        )

    def send_part(u, t, part):
        coded, scale = quantize(part)
        p_send[u, t] = coded
        p_scale_send[u, t] = scale
        for copy in part_copies(u, t):
            copy.start()

    def with_received(u, t):
        total = own[u // 2, t]
        bit = 1
        while bit < ((u & -u) or n_tp):
            v, q = u | bit, t ^ bit
            for copy in part_copies(v, q):
                copy.wait_recv()
            total = total + restore(p_recv[v, q], p_scale_recv[v, q, 0:1, 0:1])
            bit *= 2
        return total

    def forward(bit, places_of):
        for t in places_of:
            for u in range(bit, n_tp, 2 * bit):
                send_part(u, t, with_received(u, t))

    for t in range(n_tp):
        if t:
            x_copy(t).wait_recv()
        for u in range(1, n_tp, 2):
            send_part(u, t, product(t, u))
        for u in range(0, n_tp, 2):
            own[u // 2, t] = product(t, u)
        if t == 1:
            place_rows()
        if t >= 2 and t % 2 == 0:
            forward(2, (t - 2, t - 1))
    forward(2, (n_tp - 2, n_tp - 1))
    bit = 4
    while bit < n_tp:
        forward(bit, range(n_tp))
        bit *= 2

    lane = lax.broadcasted_iota(jnp.int32, (rows, 128), 1)
    lane_half = lane // rank
    slots = row_slot[...].reshape(rows, 128)
    per = 128 // rank
    l_sum = jnp.zeros((rows, 128), jnp.float32)
    for u in range(n_serve):
        if u > 0:
            panel_copy(send_a, got_a, a_send, a_recv, u, u).wait_recv()
        found = lax.dot_general(
            xs[...].reshape(rows, depth), (got_a[u] if u else send_a[0]), (((1,), (1,)), ((), ())),
            preferred_element_type=jnp.float32,
        )
        for h in range(cap // per):
            keep = slots == u * cap + h * per + lane_half
            l_sum = l_sum + jnp.where(keep, found[:, h * 128:(h + 1) * 128], 0.0)
    l_sum = l_sum + pltpu.roll(l_sum, rank, 1)
    for t in range(n_tp):
        low_rows[flip(me, t, n_tp)] = l_sum[t * block:(t + 1) * block]
    l_sum = low_rows[...].reshape(rows, 128)
    left = lax.broadcasted_iota(jnp.int32, (half, 128), 1) < rank
    packed = jnp.where(left, l_sum[:half], l_sum[half:])
    coded, scale = quantize(packed)
    l_send[...] = coded
    l_scale_send[...] = scale
    for u in range(1, n_tp):
        for copy in low_copies(u):
            copy.start()
    total = packed
    for u in range(1, n_tp):
        for copy in low_copies(u):
            copy.wait_recv()
        total = total + restore(l_recv[u], l_scale_recv[u][0:1, :])
    turned = pltpu.roll(total, rank, 1)
    low_rows[...] = jnp.concatenate(
        [jnp.where(left, total, turned), jnp.where(left, turned, total)], axis=0
    ).reshape(n_tp, block, 128)
    low = jnp.concatenate([low_rows[flip(me, t, n_tp)] for t in range(n_tp)], axis=0)

    high = low.astype(jnp.bfloat16).astype(jnp.float32)
    rest = low - high
    update = jnp.zeros((rows, feats), jnp.float32)
    for u in range(n_serve):
        if u > 0:
            panel_copy(send_b, got_b, bs_send, bs_recv, u, u).wait_recv()
        for h in range(cap // per):
            keep = slots == u * cap + h * per + lane_half
            panel = (got_b if u else send_b)[u, h * 128:(h + 1) * 128, :]
            for piece in (high, rest):
                update = update + jnp.dot(
                    jnp.where(keep, piece, 0.0).astype(jnp.bfloat16), panel,
                    preferred_element_type=jnp.float32,
                )
    own[0] = own[0] + adapter_scale * update.reshape(n_tp, block, feats)

    for t in range(n_tp):
        j = flip(me, t, n_tp)
        result = with_received(0, t)
        out[pl.ds(pl.multiple_of(j * block, block), block), :] = result.astype(jnp.bfloat16)

    for u in range(1, n_tp):
        x_copy(u).wait_send()
        for copy in low_copies(u):
            copy.wait_send()

        for t in range(n_tp):
            for copy in part_copies(u, t):
                copy.wait_send()

    for u in range(1, n_serve):
        panel_copy(send_a, got_a, a_send, a_recv, u, u).wait_send()
        panel_copy(send_b, got_b, bs_send, bs_recv, u, u).wait_send()


def body(hidden, kv_weight, a_store, b_store, home, wanted, tile_slot):
    n_tp = lax.axis_size("tp")
    n_serve = lax.axis_size("serve")
    block, width = hidden.shape
    depth = width // n_tp
    held, _, rank = a_store.shape
    feats = b_store.shape[2]
    rows = block * n_tp
    cap = max(2, (wanted.shape[1] + n_serve - 1) // n_serve)
    cap = cap + cap % 2
    panels = jnp.transpose(a_store, (0, 2, 1))
    bf16, f32, i16 = jnp.bfloat16, jnp.float32, jnp.int16
    dma = pltpu.SemaphoreType.DMA
    smem = pl.BlockSpec(memory_space=pltpu.SMEM)
    hbm = pl.BlockSpec(memory_space=pl.ANY)
    scratch = [
        pltpu.VMEM((n_tp, block, depth), bf16),
        pltpu.VMEM(kv_weight.shape, bf16),
        pltpu.VMEM(panels.shape, bf16),
        pltpu.VMEM(b_store.shape, bf16),
        pltpu.VMEM((n_serve, cap * rank, depth), bf16),
        pltpu.VMEM((n_serve, cap * rank, feats), bf16),
        pltpu.VMEM((n_serve, cap * rank, depth), bf16),
        pltpu.VMEM((n_serve, cap * rank, feats), bf16),
        pltpu.VMEM((n_tp, n_tp, block, feats), i16),
        pltpu.VMEM((n_tp, n_tp, 8, 128), f32),
        pltpu.VMEM((n_tp, n_tp, block, feats), i16),
        pltpu.VMEM((n_tp, n_tp, 8, 128), f32),
        pltpu.VMEM((rows // 2, 128), i16),
        pltpu.VMEM((8, 128), f32),
        pltpu.VMEM((n_tp, rows // 2, 128), i16),
        pltpu.VMEM((n_tp, 8, 128), f32),
        pltpu.VMEM((n_tp // 2, n_tp, block, feats), f32),
        pltpu.VMEM((n_tp, block, 128), jnp.int32),
        pltpu.VMEM((n_tp, block, 128), f32),
        pltpu.SMEM((n_serve, cap), jnp.int32),
        pltpu.SMEM((wanted.shape[1],), jnp.int32),
        dma((4,)),
        dma((n_tp,)), dma((n_tp,)),
        dma((n_serve,)), dma((n_serve,)), dma((n_serve,)), dma((n_serve,)),
        dma((n_tp, n_tp)), dma((n_tp, n_tp)), dma((n_tp, n_tp)), dma((n_tp, n_tp)),
        dma((n_tp,)), dma((n_tp,)), dma((n_tp,)), dma((n_tp,)),
    ]
    return pl.pallas_call(
        functools.partial(kernel, (n_tp, n_serve, cap, held)),
        out_shape=jax.ShapeDtypeStruct((rows, feats), bf16),
        in_specs=[smem, smem, smem, hbm, hbm, hbm, hbm],
        out_specs=pl.BlockSpec(memory_space=pltpu.VMEM),
        scratch_shapes=scratch,
        compiler_params=pltpu.CompilerParams(
            collective_id=0, has_side_effects=True, vmem_limit_bytes=56 * 1024 * 1024
        ),
    )(home, wanted, tile_slot, hidden, kv_weight, panels, b_store)


def solution(mesh):
    in_specs = (
        P(("rep", "serve", "tp"), None),
        P("tp", None),
        P("serve", "tp", None),
        P("serve", None, "tp"),
        P("rep"),
        P("rep", None),
        P(("rep", "serve")),
    )
    out_specs = P(("rep", "serve"), "tp")
    return jax.shard_map(body, mesh=mesh, in_specs=in_specs, out_specs=out_specs, check_vma=False)
```
